256 devices in a mesh: dp: 16 (over z, core), vocab: 16 (over y, x).
Axes of the slice: x: 4, y: 4, z: 8, core: 2. Of those that a mesh axis runs over, the one named last changes fastest.
Arguments:
- hidden: bfloat16 [256, 7168], P('dp'), may hold values from -400 to 400, as said below
- head_table: bfloat16 [7168, 106496], P('dp', 'vocab'), may hold values from -1 to 1
- embed_table: bfloat16 [106496, 7168], P('vocab', 'dp'), may hold values from -384 to 384
Outputs:
- next_input: bfloat16 [256, 7168], P('dp', 'vocab')
The draws below stay inside these ranges and needn't reach their ends.
Inputs may be any that keep to these rules, and one draw needn't show every extreme that they name: hidden states of a final norm.
All inputs are finite; a program needn't handle non-finite values.
Results may differ from the reference program's by a relative error of at most 0.02.
Values may be sent and summed in bfloat16 or wider, within the bound.
No kernel may reach another device: no remote copies, remote signals or barrier semaphores. Data moves between devices by JAX's collectives and lax.ppermute only.
A program may use at most 64 MiB of HBM per device.

```python
import jax
import jax.numpy as jnp

D = 7168
ROWS = 256
VOCAB = 106496


def common_parts(key):
    gauss = jnp.clip(jax.random.normal(jax.random.fold_in(key, 12), (D, VOCAB), jnp.float32), -6.0, 6.0)
    spread = 1.0 + 0.15 * jnp.arange(VOCAB, dtype=jnp.float32) / VOCAB
    table = gauss * spread[None, :] * D ** (-0.5)
    return table


def draw_head_table(key, part):
    table = common_parts(key)
    return table.astype(jnp.bfloat16)


def draw_hidden(key, part):
    key = jax.random.fold_in(key, 2)
    values = jnp.clip(jax.random.normal(jax.random.fold_in(key, 5), (ROWS, D), jnp.float32), -6.0, 6.0)
    return jnp.clip(values, -400.0, 400.0).astype(jnp.bfloat16)


def draw_embed_table(key, part):
    key = jax.random.fold_in(key, 7)
    values = jnp.clip(jax.random.normal(key, (VOCAB, D), jnp.float32), -6.0, 6.0)
    return (64.0 * values).astype(jnp.bfloat16)


def setup_inputs(seed: int = 0) -> dict:
    streams_of = jax.random.split(jax.random.key(seed), 4)
    hidden = draw_hidden(jax.random.fold_in(streams_of[3], 71), 0)
    head_table = draw_head_table(jax.random.fold_in(streams_of[3], 71), 0)
    embed_table = draw_embed_table(jax.random.fold_in(streams_of[3], 71), 0)
    return dict(hidden=hidden, head_table=head_table, embed_table=embed_table)


def reference(hidden, head_table, embed_table):
    logits = jnp.dot(hidden, head_table, preferred_element_type=jnp.float32)
    row_top = jnp.max(logits, axis=1, keepdims=True)
    scaled = jnp.exp(logits - row_top)
    row_total = jnp.sum(scaled, axis=1, keepdims=True)
    weights = scaled.astype(jnp.bfloat16)
    mixture = jnp.dot(weights, embed_table, preferred_element_type=jnp.float32)
    return (mixture / row_total).astype(jnp.bfloat16)
```

```python
import jax
import jax.numpy as jnp
from jax import lax
from jax.sharding import PartitionSpec as P

WIRE = jnp.float16
SCALE = 1.0 / 64.0
BF16, F32 = jnp.bfloat16, jnp.float32


def pieces(value, width):
    parts = []
    for _ in range(3):
        head = lax.reduce_precision(value, 8, 7)
        parts.append(head.astype(BF16))
        value = value - head
    return parts


def stat_block(top, total, width):
    block = jnp.concatenate(pieces(top, width) + pieces(total, width), -1)
    pad = [(0, 0)] * (block.ndim - 1) + [(0, width - 6)]
    return jnp.pad(block, pad)


def read_stats(block):
    block = block.astype(F32)
    top = block[..., 0:1] + block[..., 1:2] + block[..., 2:3]
    total = block[..., 3:4] + block[..., 4:5] + block[..., 5:6]
    return top, total


def on_device(hidden, head_table, embed_table):
    me = lax.axis_index("dp")
    z, core = me // 2, me % 2
    size = lax.axis_size("dp")
    chips = size // 2
    rows_dev = hidden.shape[0]
    feats, vocab = head_table.shape
    half = vocab // 2
    cut = (half // 256) * 128

    swap_pairs = [(i, i ^ 1) for i in range(size)]
    up_pairs = [(i, (i + 2) % size) for i in range(size)]
    down_pairs = [(i, (i - 2) % size) for i in range(size)]
    swap = lambda x: lax.ppermute(x, "dp", swap_pairs)
    up = lambda x: lax.ppermute(x, "dp", up_pairs)
    down = lambda x: lax.ppermute(x, "dp", down_pairs)
    dot = lambda a, b: jnp.dot(a, b, preferred_element_type=F32)
    enc = lambda x: (x * SCALE).astype(WIRE)
    dec = lambda x: x.astype(F32) * (1.0 / SCALE)

    mine, other = core * half, (1 - core) * half
    slices = lax.all_to_all(hidden, "dp", split_axis=1, concat_axis=0, tiled=True)
    head_other = swap(lax.dynamic_slice_in_dim(head_table, other, half, 1))
    slices_other = swap(slices)
    embed_other = swap(lax.dynamic_slice_in_dim(embed_table, other, half, 0))
    head_mine = lax.dynamic_slice_in_dim(head_table, mine, half, 1)
    embed_mine = lax.dynamic_slice_in_dim(embed_table, mine, half, 0)

    def batch_rows(x, b):
        return x.reshape(chips, 2, rows_dev, feats)[:, b].reshape(chips * rows_dev, feats)

    def ring_sum(logits):
        part = lambda o: lax.dynamic_index_in_dim(logits, (z + o) % chips, 0, keepdims=False)
        far = part(4)
        a = up(enc(far[:, :cut]))
        b = down(enc(far[:, cut:]))
        p3, m3 = part(3), part(-3)
        a = up(enc(jnp.concatenate([p3[:, :cut] + dec(a), p3[:, cut:]], 1)))
        b = down(enc(jnp.concatenate([m3[:, :cut], m3[:, cut:] + dec(b)], 1)))
        a = up(enc(part(2) + dec(a)))
        b = down(enc(part(-2) + dec(b)))
        a = up(enc(part(1) + dec(a)))
        b = down(enc(part(-1) + dec(b)))
        return part(0) + dec(a) + dec(b)

    def ring_gather(block):
        buf = jnp.zeros((chips,) + block.shape, block.dtype)
        put = lambda buf, x, o, c: lax.dynamic_update_slice(buf, x[None], ((z + o) % chips, 0, c))
        buf = put(buf, block, 0, 0)
        a, b = block, block
        for step in range(1, 4):
            a, b = up(a), down(b)
            buf = put(put(buf, a, -step, 0), b, step, 0)
        a, b = up(a[:, :cut]), down(b[:, cut:])
        buf = put(put(buf, a, -4, 0), b, 4, cut)
        return buf.reshape(chips * block.shape[0], block.shape[1])

    outs = []
    for b in range(2):
        logits = dot(batch_rows(slices, b), head_mine) + dot(batch_rows(slices_other, b), head_other)
        full = ring_sum(logits.reshape(chips, rows_dev, half))
        top = jnp.max(full, axis=1, keepdims=True)
        scaled = jnp.exp(full - top)
        total = jnp.sum(scaled, axis=1, keepdims=True)
        block = jnp.concatenate([scaled.astype(BF16), stat_block(top, total, 128)], 1)
        block = ring_gather(block)
        weights, stats = block[:, :half], block[:, half : half + 64]
        value_other = dot(weights, embed_other).astype(BF16)
        from_other = swap(jnp.concatenate([value_other, stats], 1))
        value_mine = dot(weights, embed_mine)
        top_m, tot_m = read_stats(stats)
        top_o, tot_o = read_stats(from_other[:, feats:])
        top = jnp.maximum(top_m, top_o)
        f_m, f_o = jnp.exp(top_m - top), jnp.exp(top_o - top)
        value = value_mine * f_m + from_other[:, :feats].astype(F32) * f_o
        out = jnp.concatenate([value.astype(BF16), stat_block(top, tot_m * f_m + tot_o * f_o, 64)], 1)
        outs.append(out.reshape(chips, rows_dev, feats + 64))

    blocks = jnp.stack(outs, 1).reshape(size, rows_dev, feats + 64)
    got = lax.all_to_all(blocks, "vocab", 0, 0)
    tops, tots = read_stats(got[:, :, feats:])
    factor = jnp.exp(tops - jnp.max(tops, axis=0, keepdims=True))
    row_total = jnp.sum(tots * factor, axis=0)
    mixture = jnp.sum(got[:, :, :feats].astype(F32) * factor, axis=0)
    result = (mixture / row_total).astype(BF16)
    flip = [(d * size + v, v * size + d) for d in range(size) for v in range(size)]
    return lax.ppermute(result, ("dp", "vocab"), flip)


def solution(mesh):
    in_specs = (P("dp", None), P("dp", "vocab"), P("vocab", "dp"))
    out_specs = P("dp", "vocab")
    return jax.shard_map(
        on_device, mesh=mesh, in_specs=in_specs, out_specs=out_specs, check_vma=False
    )
```

```python
import jax
import jax.numpy as jnp
from jax import lax
from jax.sharding import PartitionSpec as P

WIRE = jnp.float16
SCALE = 1.0 / 64.0
BF16, F32 = jnp.bfloat16, jnp.float32
STAT = 128


def pieces(value):
    parts = []
    for _ in range(3):
        head = lax.reduce_precision(value, 8, 7)
        parts.append(head.astype(BF16))
        value = value - head
    return parts


def stat_block(top, total):
    block = jnp.concatenate(pieces(top) + pieces(total), -1)
    return jnp.pad(block, [(0, 0)] * (block.ndim - 1) + [(0, STAT - 6)])


def read_stats(block):
    block = block.astype(F32)
    top = block[..., 0:1] + block[..., 1:2] + block[..., 2:3]
    total = block[..., 3:4] + block[..., 4:5] + block[..., 5:6]
    return top, total


def on_device(hidden, head_table, embed_table):
    me = lax.axis_index("dp")
    z, core = me // 2, me % 2
    size = lax.axis_size("dp")
    chips = size // 2
    rows_dev = hidden.shape[0]
    feats, vocab = head_table.shape
    cut = (vocab // 256) * 128

    swap = lambda x: lax.ppermute(x, "dp", [(i, i ^ 1) for i in range(size)])
    up = lambda x: lax.ppermute(x, "dp", [(i, (i + 2) % size) for i in range(size)])
    down = lambda x: lax.ppermute(x, "dp", [(i, (i - 2) % size) for i in range(size)])
    dot = lambda a, b: jnp.dot(a, b, preferred_element_type=F32)
    enc = lambda x: (x * SCALE).astype(WIRE)
    dec = lambda x: x.astype(F32) * (1.0 / SCALE)

    groups = [[c + 2 * k for k in range(chips)] for c in range(2)]
    slices = lax.all_to_all(
        hidden, "dp", split_axis=1, concat_axis=0, tiled=True, axis_index_groups=groups
    )
    head_other = swap(head_table)
    embed_other = swap(embed_table)
    slices = jnp.roll(slices.reshape(chips, rows_dev, 2 * feats), -z, 0)
    first, second = slices[:, :, :feats], slices[:, :, feats:]
    own = jnp.where(core == 0, first, second).reshape(chips * rows_dev, feats)
    others = jnp.where(core == 0, second, first).reshape(chips * rows_dev, feats)

    logits = dot(own, head_table) + dot(others, head_other)
    logits = logits.reshape(chips, rows_dev, vocab)
    part = lambda o: logits[o % chips]

    far = part(4)
    a, b = up(enc(far[:, :cut])), down(enc(far[:, cut:]))
    p3, m3 = part(3), part(-3)
    a = up(enc(jnp.concatenate([p3[:, :cut] + dec(a), p3[:, cut:]], 1)))
    b = down(enc(jnp.concatenate([m3[:, :cut], m3[:, cut:] + dec(b)], 1)))
    a, b = up(enc(part(2) + dec(a))), down(enc(part(-2) + dec(b)))
    a, b = up(enc(part(1) + dec(a))), down(enc(part(-1) + dec(b)))
    full = part(0) + dec(a) + dec(b)

    top = jnp.max(full, axis=1, keepdims=True)
    scaled = jnp.exp(full - top)
    total = jnp.sum(scaled, axis=1, keepdims=True)
    block = jnp.concatenate([scaled.astype(BF16), stat_block(top, total)], 1)

    got = {0: block}
    a, b = block, block
    for step in range(1, 4):
        a, b = up(a), down(b)
        got[chips - step], got[step] = a, b
    a, b = up(a[:, :cut]), down(b[:, cut:])
    got[4] = jnp.concatenate([a, b], 1)

    def mix(order):
        block = jnp.concatenate([got[o] for o in order], 0)
        weights, stats = block[:, :vocab], block[:, vocab:]
        return dot(weights, embed_table).astype(BF16), dot(weights, embed_other).astype(BF16), stats

    early = mix([6, 7, 0, 1, 2])
    late = mix([3, 4, 5])
    value_own, value_other, stats = [jnp.concatenate([e, l], 0) for e, l in zip(early, late)]
    first = jnp.where(core == 0, value_own, value_other)
    second = jnp.where(core == 0, value_other, value_own)
    shape = lambda x: x.reshape(chips, rows_dev, x.shape[-1])
    first, second, stats = shape(first), shape(second), shape(stats)
    blocks = jnp.stack(
        [jnp.concatenate([first, stats], 2), jnp.concatenate([second, stats], 2)], 1
    )
    blocks = jnp.roll(blocks, z - 2, 0).reshape(size, rows_dev, feats + STAT)

    got = lax.all_to_all(blocks, "vocab", 0, 0)
    tops, tots = read_stats(got[:, :, feats:])
    factor = jnp.exp(tops - jnp.max(tops, axis=0, keepdims=True))
    row_total = jnp.sum(tots * factor, axis=0)
    mixture = jnp.sum(got[:, :, :feats].astype(F32) * factor, axis=0)
    result = (mixture / row_total).astype(BF16)
    flip = []
    for k in range(chips):
        for c in range(2):
            for r in range(chips):
                for f in range(2):
                    here = (2 * k + c) * size + 2 * r + f
                    there = (2 * r + c) * size + 2 * k + f
                    flip.append((here, there))
    return lax.ppermute(result, ("dp", "vocab"), flip)


def solution(mesh):
    in_specs = (P("dp", None), P("dp", "vocab"), P("vocab", "dp"))
    out_specs = P("dp", "vocab")
    return jax.shard_map(
        on_device, mesh=mesh, in_specs=in_specs, out_specs=out_specs, check_vma=False
    )
```

```python
import jax
import jax.numpy as jnp
from jax import lax
from jax.experimental import pallas as pl
from jax.experimental.pallas import tpu as pltpu
from jax.sharding import PartitionSpec as P

BF16, F32 = jnp.bfloat16, jnp.float32
WIRE = jnp.float16
SCALE = 1.0 / 64.0
TILE, HALF = 128, 64
LOW = -3.0e38
PLACE = [7, 2, 11, 6, 3, 14, 12, 13, 0, 1, 4, 5, 15, 9, 8, 10]


def place(z, r, f):
    rel = PLACE[2 * ((r - z) % 8) + f]
    return (z // 2 + rel // 4) % 4 * 4 + (2 * z + rel) % 4

VMEM = pl.BlockSpec(memory_space=pltpu.VMEM)
HBM = pl.BlockSpec(memory_space=pltpu.HBM)
stay = lambda x: pltpu.with_memory_space_constraint(x, pltpu.HBM)
limit = pltpu.CompilerParams(vmem_limit_bytes=16 << 20)
iota = lambda rows: lax.broadcasted_iota(jnp.int32, (rows, TILE), 1)


def here():
    me = lax.axis_index("dp")
    return me >> 1, me & 1


def chunk_of(d):
    z, core = here()
    return (z + (1 - 2 * core) * d) & 7


def window(d, width):
    chunk, half = chunk_of(d), width // TILE - 1
    start = ((2 * half + 1) * (chunk >> 1) + half * (chunk & 1)) * TILE
    return pl.ds(pl.multiple_of(start, TILE), width)


def cost(flops, size):
    return pl.CostEstimate(flops=flops, bytes_accessed=size, transcendentals=0)


def pieces(value):
    parts = []
    for _ in range(3):
        head = value.astype(BF16)
        parts.append(head)
        value = value - head.astype(F32)
    return parts


def stat_lanes(top, total, rows):
    lane = iota(rows) % HALF
    out = jnp.zeros((rows, TILE), F32)
    for i, piece in enumerate(pieces(top) + pieces(total)):
        out = jnp.where(lane == i, piece.astype(F32), out)
    return out


def read_lanes(tile, lane):
    top = jnp.sum(jnp.where((lane >= 0) & (lane < 3), tile, 0.0), axis=-1, keepdims=True)
    total = jnp.sum(jnp.where((lane >= 3) & (lane < 6), tile, 0.0), axis=-1, keepdims=True)
    return top, total


def deal_kernel(hidden_ref, out_ref, sem):
    width = out_ref.shape[2]
    copies = [
        pltpu.make_async_copy(hidden_ref.at[:, k * width : (k + 1) * width], out_ref.at[k], sem.at[k])
        for k in range(out_ref.shape[0])
    ]
    for copy in copies:
        copy.start()
    for copy in copies:
        copy.wait()


def deal(hidden, parts):
    rows, feats = hidden.shape
    return pl.pallas_call(
        deal_kernel,
        out_shape=jax.ShapeDtypeStruct((parts, rows, feats // parts), BF16),
        in_specs=[HBM],
        out_specs=VMEM,
        scratch_shapes=[pltpu.SemaphoreType.DMA((parts,))],
        cost_estimate=cost(0, 1 << 19),
        compiler_params=limit,
        name="deal",
    )(stay(hidden))


def logits_kernel(order, own_ref, other_ref, *refs):
    tables, outs, (buf, sem) = refs[:2], refs[2:-2], refs[-2:]
    width = outs[0].shape[1]
    copies = [
        [
            pltpu.make_async_copy(t.at[:, window(d, width)], buf.at[slot, k], sem.at[slot, k])
            for k, t in enumerate(tables)
        ]
        for slot, d in enumerate(order)
    ]
    for pair in copies:
        for copy in pair:
            copy.start()
    for slot in range(len(order)):
        copies[slot][0].wait()
        part = jnp.dot(own_ref[...], buf[slot, 0], preferred_element_type=F32)
        copies[slot][1].wait()
        outs[slot][...] = part + jnp.dot(other_ref[...], buf[slot, 1], preferred_element_type=F32)


def logits_of(order, own, other, tables, width):
    rows, feats = own.shape
    n = len(order)
    return pl.pallas_call(
        lambda *refs: logits_kernel(order, *refs),
        out_shape=[jax.ShapeDtypeStruct((rows, width), F32)] * n,
        in_specs=[VMEM] * 2 + [HBM] * 2,
        out_specs=[VMEM] * n,
        scratch_shapes=[
            pltpu.VMEM((n, 2, feats, width), BF16),
            pltpu.SemaphoreType.DMA((n, 2)),
        ],
        cost_estimate=cost(4 * n * rows * feats * width, 4 * n * feats * width),
        compiler_params=limit,
        name=f"logits{n}",
    )(own, other, *[stay(t) for t in tables])


def softmax_kernel(full_ref, unused_ref, out_ref):
    rows, width = full_ref.shape
    odd = (chunk_of(0) & 1) == 1
    last = width - TILE
    lane = iota(rows)
    mine0 = jnp.logical_or(lane >= HALF, jnp.logical_not(odd))
    mine6 = jnp.logical_or(lane < HALF, odd)
    tile0 = jnp.where(mine0, full_ref[:, :TILE], LOW)
    tile6 = jnp.where(mine6, full_ref[:, last:], LOW)
    mid = full_ref[:, TILE:last]
    biggest = lambda x: jnp.max(x, axis=1, keepdims=True)
    top = jnp.maximum(biggest(mid), biggest(jnp.maximum(tile0, tile6)))
    mid = jnp.exp(mid - top)
    tile0 = jnp.where(mine0, jnp.exp(tile0 - top), 0.0)
    tile6 = jnp.where(mine6, jnp.exp(tile6 - top), 0.0)
    total = jnp.sum(mid, axis=1, keepdims=True) + jnp.sum(tile0 + tile6, axis=1, keepdims=True)
    stats = stat_lanes(top, total, rows)
    out_ref[:, :TILE] = jnp.where(mine0, tile0, stats).astype(BF16)
    out_ref[:, TILE:last] = mid.astype(BF16)
    out_ref[:, last:] = jnp.where(mine6, tile6, stats).astype(BF16)


def softmax_of(full, embed_other):
    return pl.pallas_call(
        softmax_kernel,
        out_shape=jax.ShapeDtypeStruct(full.shape, BF16),
        in_specs=[VMEM, HBM],
        out_specs=VMEM,
        cost_estimate=cost(1 << 20, 1 << 20),
        compiler_params=limit,
        name="softmax",
    )(full, stay(embed_other))


def mix_kernel(order, ahead, n_in, *refs):
    first, last = order == (0,), 4 in order
    blocks, refs = refs[:n_in], refs[n_in:]
    if last:
        (ready_ref, old_ref, old_stat_ref), (out_ref, w_ref, ship_ref) = refs[:3], refs[3:]
    else:
        tables, refs = refs[:2], refs[2:]
        if not first:
            old_ref, old_stat_ref, refs = refs[0], refs[1], refs[2:]
        out_ref, stat_ref, zero_ref, zero2_ref, refs = *refs[:4], refs[4:]
        if ahead:
            ahead_ref, refs = refs[0], refs[1:]
        w_ref, ready_ref, sem = refs
    n, rows, width = w_ref.shape
    feats = ready_ref.shape[2]
    nt = lambda a, b: lax.dot_general(a, b, (((1,), (1,)), ((), ())), preferred_element_type=F32)
    lane = iota(rows)
    tail = width - TILE

    def copies(d, to, slot):
        return [
            pltpu.make_async_copy(tables[k].at[:, window(d, width)], to.at[k], sem.at[slot, k])
            for k in range(2)
        ]

    now, later = [], []
    if not last:
        now = [copies(d, ready_ref.at[slot], slot) for slot, d in enumerate(order)]
        later = [c for k, d in enumerate(ahead) for c in copies(d, ahead_ref.at[k], n + k)]
    for copy in [c for pair in now for c in pair] + later:
        copy.start()
    sums, tops, totals = [], [], []
    for slot, d in enumerate(order):
        w_ref[slot] = blocks[slot][...]
        odd = (chunk_of(d) & 1) == 1
        tile0, tile6 = w_ref[slot, :, :TILE].astype(F32), w_ref[slot, :, tail:].astype(F32)
        top, total = read_lanes(jnp.where(odd, tile0, tile6), lane - jnp.where(odd, 0, HALF))
        tops.append(top)
        totals.append(total)
        low = jnp.logical_and(odd, lane < HALF)
        high = jnp.logical_and(jnp.logical_not(odd), lane >= HALF)
        w_ref[slot, :, :TILE] = jnp.where(low, 0.0, tile0).astype(BF16)
        w_ref[slot, :, tail:] = jnp.where(high, 0.0, tile6).astype(BF16)
    for slot in range(n):
        for copy in now[slot] if now else []:
            copy.wait()
        sums.append([nt(w_ref[slot], ready_ref[slot, k]) for k in range(2)])
    if not first:
        tops.append(old_stat_ref[:, 0:1])
        totals.append(old_stat_ref[:, 1:2])
        sums.append((old_ref[0, :, :feats], old_ref[1, :, :feats]))
    top = tops[0]
    for t in tops[1:]:
        top = jnp.maximum(top, t)
    factors = [jnp.exp(t - top) for t in tops]
    total = sum(t * f for t, f in zip(totals, factors))
    mine, others = [sum(s[k] * f for s, f in zip(sums, factors)) for k in range(2)]
    if not last:
        out_ref[0, :, :feats] = mine
        out_ref[1, :, :feats] = others
        stat_ref[...] = jnp.where(lane == 0, top, total)
        zero_ref[...] = jnp.zeros_like(zero_ref)
        zero2_ref[...] = jnp.zeros_like(zero2_ref)
        for copy in later:
            copy.wait()
        return
    stats = stat_lanes(top, total, rows)
    z, core = here()
    cut = feats // TILE * TILE
    for k, value in enumerate((mine, others)):
        ship_ref[k, :, :cut] = value[:, :cut].astype(BF16)
        ship_ref[k, :, cut:] = jnp.concatenate(
            [value[:, cut:], stats[:, : TILE - (feats - cut)]], 1
        ).astype(BF16)
    for dz in range(8):
        at = pl.ds(pl.multiple_of(((z + dz) & 7) * 16, 16), 16)
        spots = [((z >> 1) + rel // 4 & 3) * 4 + (2 * z + rel % 4 & 3) for rel in PLACE[2 * dz : 2 * dz + 2]]
        out_ref[jnp.where(core == 0, spots[0], spots[1])] = ship_ref[0, at, :]
        out_ref[jnp.where(core == 0, spots[1], spots[0])] = ship_ref[1, at, :]


def mix_of(order, blocks, tables, ready, old, ahead=()):
    n, last = len(order), 4 in order
    rows, width = blocks[0].shape
    feats = tables[0].shape[0]
    wide = pl.cdiv(feats, TILE) * TILE
    scratch = [pltpu.VMEM((n, rows, width), BF16)]
    if last:
        tables = []
        out_shape = [jax.ShapeDtypeStruct((rows // 8, 16, wide), BF16)]
        scratch.append(pltpu.VMEM((2, rows, wide), BF16))
    else:
        out_shape = [
            jax.ShapeDtypeStruct((2, rows, wide), F32),
            jax.ShapeDtypeStruct((rows, TILE), F32),
            jax.ShapeDtypeStruct((1, width), BF16),
            jax.ShapeDtypeStruct((1, width), BF16),
        ]
        if ahead:
            out_shape.append(jax.ShapeDtypeStruct((len(ahead), 2, feats, width), BF16))
        scratch.append(pltpu.VMEM((n, 2, feats, width), BF16))
        scratch.append(pltpu.SemaphoreType.DMA((n + len(ahead), 2)))
    specs = [VMEM] * len(blocks) + [HBM] * len(tables)
    return pl.pallas_call(
        lambda *refs: mix_kernel(order, ahead, len(blocks), *refs),
        out_shape=out_shape,
        in_specs=specs + [VMEM] * len(ready + old),
        out_specs=[VMEM] * len(out_shape),
        scratch_shapes=scratch,
        cost_estimate=cost(4 * n * rows * feats * width, 4 * n * feats * width),
        compiler_params=limit,
        name=f"mix{n}{'l' if last else ''}",
    )(*blocks, *[stay(t) for t in tables], *ready, *old)


def combine_kernel(got_ref, out_ref):
    parts, rows, wide = got_ref.shape
    feats = out_ref.shape[1]
    lane = iota(rows) - (feats - (wide - TILE))
    stats = [read_lanes(got_ref[v, :, wide - TILE :].astype(F32), lane) for v in range(parts)]
    top = stats[0][0]
    for t, _ in stats[1:]:
        top = jnp.maximum(top, t)
    factors = [jnp.exp(t - top) for t, _ in stats]
    total = sum(t * f for (_, t), f in zip(stats, factors))
    mixture = sum(got_ref[v].astype(F32) * f for v, f in enumerate(factors))
    out_ref[...] = (mixture / total)[:, :feats].astype(BF16)


def combine(got, feats):
    return pl.pallas_call(
        combine_kernel,
        out_shape=jax.ShapeDtypeStruct((got.shape[1], feats), BF16),
        in_specs=[VMEM],
        out_specs=VMEM,
        cost_estimate=cost(1 << 18, 1 << 18),
        compiler_params=limit,
        name="combine",
    )(got)


def on_device(hidden, head_table, embed_table):
    me = lax.axis_index("dp")
    z, core = me // 2, me % 2
    size = lax.axis_size("dp")
    chips = size // 2
    rows_dev = hidden.shape[0]
    feats, vocab = head_table.shape
    rows = chips * rows_dev
    pair = vocab // TILE // (chips // 2)
    width = (pair // 2 + 1) * TILE

    swap = lambda x: lax.ppermute(x, "dp", [(i, i ^ 1) for i in range(size)])
    side = [2 - 4 * (i % 2) for i in range(size)]
    up = lambda x: lax.ppermute(x, "dp", [(i, (i + side[i]) % size) for i in range(size)])
    down = lambda x: lax.ppermute(x, "dp", [(i, (i - side[i]) % size) for i in range(size)])
    up2 = lambda x: lax.ppermute(x, "dp", [(i, (i + 2 * side[i]) % size) for i in range(size)])
    enc = lambda x: (x * SCALE).astype(WIRE)
    dec = lambda x: x.astype(F32) * (1.0 / SCALE)

    groups = [[c + 2 * k for k in range(chips)] for c in range(2)]
    slices = lax.all_to_all(deal(hidden, chips), "dp", 0, 0, axis_index_groups=groups)
    slices = slices.reshape(rows, 2 * feats)
    head_other = swap(head_table)
    embed_own = embed_table.T
    embed_other = swap(embed_own)
    first, second = slices[:, :feats], slices[:, feats:]
    own = jnp.where(core == 0, first, second)
    others = jnp.where(core == 0, second, first)

    logits = lambda order: logits_of(order, own, others, [head_table, head_other], width)
    far, p3, m3 = logits((4, 3, 5))
    a4, a, b = up2(enc(far)), up(enc(p3)), down(enc(m3))
    p2, m2, p1, m1, p0 = logits((2, 6, 1, 7, 0))
    a = up(enc(p2 + dec(a) + dec(a4)))
    b = down(enc(m2 + dec(b)))
    a = up(enc(p1 + dec(a)))
    b = down(enc(m1 + dec(b)))
    full = p0 + dec(a) + dec(b)

    block = softmax_of(full, embed_other)
    tables = [embed_own, embed_other]
    mix = lambda order, blocks, old, **kw: mix_of(order, blocks, tables, [], old, **kw)
    a1 = up(block)
    *state, za, zb = mix((0,), [block], [])
    b1 = down(block + zb)
    a2 = up(a1 + za)
    *state, za, zb = mix((7,), [a1], state)
    b2 = down(b1 + zb)
    a2_sent = a2 + za
    a4, a3 = up2(a2_sent), up(a2_sent)
    b3 = down(b2)
    *state, _, _ = mix((1, 6), [b1, a2], state)
    *state, _, _, ready = mix((2, 5), [b2, a3], state, ahead=(3, 4))
    (blocks,) = mix_of((3, 4), [b3, a4], tables, [ready], state)

    result = combine(lax.all_to_all(blocks, "vocab", 0, 0), feats)
    flip = []
    for k in range(chips):
        for c in range(2):
            for r in range(chips):
                for f in range(2):
                    here = (2 * k + c) * size + place(k, r, f)
                    there = (2 * r + c) * size + 2 * k + f
                    flip.append((here, there))
    return lax.ppermute(result, ("dp", "vocab"), flip)


def solution(mesh):
    in_specs = (P("dp", None), P("dp", "vocab"), P("vocab", "dp"))
    out_specs = P("dp", "vocab")
    return jax.shard_map(
        on_device, mesh=mesh, in_specs=in_specs, out_specs=out_specs, check_vma=False
    )
```

```python
import jax
import jax.numpy as jnp
from jax import lax
from jax.experimental import pallas as pl
from jax.experimental.pallas import tpu as pltpu
from jax.sharding import PartitionSpec as P

BF16, F32 = jnp.bfloat16, jnp.float32
WIRE = jnp.float16
SCALE = 1.0 / 64.0
TILE, HALF = 128, 64
LOW = -3.0e38
PLACE = [7, 2, 11, 6, 3, 14, 12, 13, 0, 1, 4, 5, 15, 9, 8, 10]


def place(z, r, f):
    rel = PLACE[2 * ((r - z) % 8) + f]
    return (z // 2 + rel // 4) % 4 * 4 + (2 * z + rel) % 4

VMEM = pl.BlockSpec(memory_space=pltpu.VMEM)
HBM = pl.BlockSpec(memory_space=pltpu.HBM)
stay = lambda x: pltpu.with_memory_space_constraint(x, pltpu.HBM)
limit = pltpu.CompilerParams(vmem_limit_bytes=16 << 20)
iota = lambda rows: lax.broadcasted_iota(jnp.int32, (rows, TILE), 1)


def here():
    me = lax.axis_index("dp")
    return me >> 1, me & 1


def chunk_of(d):
    z, core = here()
    return (z + (1 - 2 * core) * d) & 7


def window(d, width):
    chunk, half = chunk_of(d), width // TILE - 1
    start = ((2 * half + 1) * (chunk >> 1) + half * (chunk & 1)) * TILE
    return pl.ds(pl.multiple_of(start, TILE), width)


def cost(flops, size):
    return pl.CostEstimate(flops=flops, bytes_accessed=size, transcendentals=0)


def pieces(value):
    parts = []
    for _ in range(3):
        head = value.astype(BF16)
        parts.append(head)
        value = value - head.astype(F32)
    return parts


def stat_lanes(top, total, rows):
    lane = iota(rows) % HALF
    out = jnp.zeros((rows, TILE), F32)
    for i, piece in enumerate(pieces(top) + pieces(total)):
        out = jnp.where(lane == i, piece.astype(F32), out)
    return out


def read_lanes(tile, lane):
    top = jnp.sum(jnp.where((lane >= 0) & (lane < 3), tile, 0.0), axis=-1, keepdims=True)
    total = jnp.sum(jnp.where((lane >= 3) & (lane < 6), tile, 0.0), axis=-1, keepdims=True)
    return top, total


def deal_kernel(hidden_ref, out_ref, sem):
    width = out_ref.shape[2]
    copies = [
        pltpu.make_async_copy(hidden_ref.at[:, k * width : (k + 1) * width], out_ref.at[k], sem.at[k])
        for k in range(out_ref.shape[0])
    ]
    for copy in copies:
        copy.start()
    for copy in copies:
        copy.wait()


def deal(hidden, parts):
    rows, feats = hidden.shape
    return pl.pallas_call(
        deal_kernel,
        out_shape=jax.ShapeDtypeStruct((parts, rows, feats // parts), BF16),
        in_specs=[HBM],
        out_specs=VMEM,
        scratch_shapes=[pltpu.SemaphoreType.DMA((parts,))],
        cost_estimate=cost(0, 1 << 19),
        compiler_params=limit,
        name="deal",
    )(stay(hidden))


def logits_kernel(order, own_ref, other_ref, *refs):
    tables, outs, (buf, sem) = refs[:2], refs[2:-2], refs[-2:]
    width = outs[0].shape[1]
    copies = [
        [
            pltpu.make_async_copy(t.at[:, window(d, width)], buf.at[slot, k], sem.at[slot, k])
            for k, t in enumerate(tables)
        ]
        for slot, d in enumerate(order)
    ]
    for pair in copies:
        for copy in pair:
            copy.start()
    for slot in range(len(order)):
        copies[slot][0].wait()
        part = jnp.dot(own_ref[...], buf[slot, 0], preferred_element_type=F32)
        copies[slot][1].wait()
        outs[slot][...] = part + jnp.dot(other_ref[...], buf[slot, 1], preferred_element_type=F32)


def logits_of(order, own, other, tables, width):
    rows, feats = own.shape
    n = len(order)
    return pl.pallas_call(
        lambda *refs: logits_kernel(order, *refs),
        out_shape=[jax.ShapeDtypeStruct((rows, width), F32)] * n,
        in_specs=[VMEM] * 2 + [HBM] * 2,
        out_specs=[VMEM] * n,
        scratch_shapes=[
            pltpu.VMEM((n, 2, feats, width), BF16),
            pltpu.SemaphoreType.DMA((n, 2)),
        ],
        cost_estimate=cost(4 * n * rows * feats * width, 4 * n * feats * width),
        compiler_params=limit,
        name=f"logits{n}",
    )(own, other, *[stay(t) for t in tables])


def softmax_kernel(full_ref, unused_ref, out_ref):
    rows, width = full_ref.shape
    odd = (chunk_of(0) & 1) == 1
    last = width - TILE
    lane = iota(rows)
    mine0 = jnp.logical_or(lane >= HALF, jnp.logical_not(odd))
    mine6 = jnp.logical_or(lane < HALF, odd)
    tile0 = jnp.where(mine0, full_ref[:, :TILE], LOW)
    tile6 = jnp.where(mine6, full_ref[:, last:], LOW)
    mid = full_ref[:, TILE:last]
    biggest = lambda x: jnp.max(x, axis=1, keepdims=True)
    top = jnp.maximum(biggest(mid), biggest(jnp.maximum(tile0, tile6)))
    mid = jnp.exp(mid - top)
    tile0 = jnp.where(mine0, jnp.exp(tile0 - top), 0.0)
    tile6 = jnp.where(mine6, jnp.exp(tile6 - top), 0.0)
    total = jnp.sum(mid, axis=1, keepdims=True) + jnp.sum(tile0 + tile6, axis=1, keepdims=True)
    stats = stat_lanes(top, total, rows)
    out_ref[:, :TILE] = jnp.where(mine0, tile0, stats).astype(BF16)
    out_ref[:, TILE:last] = mid.astype(BF16)
    out_ref[:, last:] = jnp.where(mine6, tile6, stats).astype(BF16)


def softmax_of(full, embed_other):
    return pl.pallas_call(
        softmax_kernel,
        out_shape=jax.ShapeDtypeStruct(full.shape, BF16),
        in_specs=[VMEM, HBM],
        out_specs=VMEM,
        cost_estimate=cost(1 << 20, 1 << 20),
        compiler_params=limit,
        name="softmax",
    )(full, stay(embed_other))


def mix_kernel(order, ahead, n_in, *refs):
    first, last = order == (0,), 4 in order
    blocks, refs = refs[:n_in], refs[n_in:]
    if last:
        (ready_ref, old_ref, old_stat_ref), (out_ref, w_ref, ship_ref) = refs[:3], refs[3:]
    else:
        tables, refs = refs[:2], refs[2:]
        if not first:
            old_ref, old_stat_ref, refs = refs[0], refs[1], refs[2:]
        out_ref, stat_ref, zero_ref, zero2_ref, refs = *refs[:4], refs[4:]
        if ahead:
            ahead_ref, refs = refs[0], refs[1:]
        w_ref, ready_ref, sem = refs
    n, rows, width = w_ref.shape
    feats = ready_ref.shape[2]
    nt = lambda a, b: lax.dot_general(a, b, (((1,), (1,)), ((), ())), preferred_element_type=F32)
    lane = iota(rows)
    tail = width - TILE

    def copies(d, to, slot):
        return [
            pltpu.make_async_copy(tables[k].at[:, window(d, width)], to.at[k], sem.at[slot, k])
            for k in range(2)
        ]

    now, later = [], []
    if not last:
        now = [copies(d, ready_ref.at[slot], slot) for slot, d in enumerate(order)]
        later = [c for k, d in enumerate(ahead) for c in copies(d, ahead_ref.at[k], n + k)]
    for copy in [c for pair in now for c in pair] + later:
        copy.start()
    sums, tops, totals = [], [], []
    for slot, d in enumerate(order):
        w_ref[slot] = blocks[slot][...]
        odd = (chunk_of(d) & 1) == 1
        tile0, tile6 = w_ref[slot, :, :TILE].astype(F32), w_ref[slot, :, tail:].astype(F32)
        top, total = read_lanes(jnp.where(odd, tile0, tile6), lane - jnp.where(odd, 0, HALF))
        tops.append(top)
        totals.append(total)
        low = jnp.logical_and(odd, lane < HALF)
        high = jnp.logical_and(jnp.logical_not(odd), lane >= HALF)
        w_ref[slot, :, :TILE] = jnp.where(low, 0.0, tile0).astype(BF16)
        w_ref[slot, :, tail:] = jnp.where(high, 0.0, tile6).astype(BF16)
    for slot in range(n):
        for copy in now[slot] if now else []:
            copy.wait()
        sums.append([nt(w_ref[slot], ready_ref[slot, k]) for k in range(2)])
    if not first:
        tops.append(old_stat_ref[:, 0:1])
        totals.append(old_stat_ref[:, 1:2])
        sums.append((old_ref[0, :, :feats], old_ref[1, :, :feats]))
    top = tops[0]
    for t in tops[1:]:
        top = jnp.maximum(top, t)
    factors = [jnp.exp(t - top) for t in tops]
    total = sum(t * f for t, f in zip(totals, factors))
    mine, others = [sum(s[k] * f for s, f in zip(sums, factors)) for k in range(2)]
    if not last:
        out_ref[0, :, :feats] = mine
        out_ref[1, :, :feats] = others
        stat_ref[...] = jnp.where(lane == 0, top, total)
        zero_ref[...] = jnp.zeros_like(zero_ref)
        zero2_ref[...] = jnp.zeros_like(zero2_ref)
        for copy in later:
            copy.wait()
        return
    stats = stat_lanes(top, total, rows)
    z, core = here()
    cut = feats // TILE * TILE
    for k, value in enumerate((mine, others)):
        ship_ref[k, :, :cut] = value[:, :cut].astype(BF16)
        ship_ref[k, :, cut:] = jnp.concatenate(
            [value[:, cut:], stats[:, : TILE - (feats - cut)]], 1
        ).astype(BF16)
    for dz in range(8):
        at = pl.ds(pl.multiple_of(((z + dz) & 7) * 16, 16), 16)
        spots = [((z >> 1) + rel // 4 & 3) * 4 + (2 * z + rel % 4 & 3) for rel in PLACE[2 * dz : 2 * dz + 2]]
        out_ref[jnp.where(core == 0, spots[0], spots[1])] = ship_ref[0, at, :]
        out_ref[jnp.where(core == 0, spots[1], spots[0])] = ship_ref[1, at, :]


def mix_of(order, blocks, tables, ready, old, ahead=()):
    n, last = len(order), 4 in order
    rows, width = blocks[0].shape
    feats = tables[0].shape[0]
    wide = pl.cdiv(feats, TILE) * TILE
    scratch = [pltpu.VMEM((n, rows, width), BF16)]
    if last:
        tables = []
        out_shape = [jax.ShapeDtypeStruct((rows // 8, 16, wide), BF16)]
        scratch.append(pltpu.VMEM((2, rows, wide), BF16))
    else:
        out_shape = [
            jax.ShapeDtypeStruct((2, rows, wide), F32),
            jax.ShapeDtypeStruct((rows, TILE), F32),
            jax.ShapeDtypeStruct((1, width), BF16),
            jax.ShapeDtypeStruct((1, width), BF16),
        ]
        if ahead:
            out_shape.append(jax.ShapeDtypeStruct((len(ahead), 2, feats, width), BF16))
        scratch.append(pltpu.VMEM((n, 2, feats, width), BF16))
        scratch.append(pltpu.SemaphoreType.DMA((n + len(ahead), 2)))
    specs = [VMEM] * len(blocks) + [HBM] * len(tables)
    return pl.pallas_call(
        lambda *refs: mix_kernel(order, ahead, len(blocks), *refs),
        out_shape=out_shape,
        in_specs=specs + [VMEM] * len(ready + old),
        out_specs=[VMEM] * len(out_shape),
        scratch_shapes=scratch,
        cost_estimate=cost(4 * n * rows * feats * width, 4 * n * feats * width),
        compiler_params=limit,
        name=f"mix{n}{'l' if last else ''}",
    )(*blocks, *[stay(t) for t in tables], *ready, *old)


def add_kernel(x_ref, y_ref, out_ref):
    out_ref[...] = x_ref[...] + y_ref[...]


def add(x, y):
    return pl.pallas_call(
        add_kernel,
        out_shape=jax.ShapeDtypeStruct(x.shape, x.dtype),
        in_specs=[VMEM] * 2,
        out_specs=VMEM,
        cost_estimate=cost(10 << 30, 1 << 20),
        compiler_params=limit,
        name="add",
    )(x, y)


def combine_kernel(got_ref, out_ref):
    parts, rows, wide = got_ref.shape
    feats = out_ref.shape[1]
    lane = iota(rows) - (feats - (wide - TILE))
    stats = [read_lanes(got_ref[v, :, wide - TILE :].astype(F32), lane) for v in range(parts)]
    top = stats[0][0]
    for t, _ in stats[1:]:
        top = jnp.maximum(top, t)
    factors = [jnp.exp(t - top) for t, _ in stats]
    total = sum(t * f for (_, t), f in zip(stats, factors))
    mixture = sum(got_ref[v].astype(F32) * f for v, f in enumerate(factors))
    out_ref[...] = (mixture / total)[:, :feats].astype(BF16)


def combine(got, feats):
    return pl.pallas_call(
        combine_kernel,
        out_shape=jax.ShapeDtypeStruct((got.shape[1], feats), BF16),
        in_specs=[VMEM],
        out_specs=VMEM,
        cost_estimate=cost(1 << 18, 1 << 18),
        compiler_params=limit,
        name="combine",
    )(got)


def on_device(hidden, head_table, embed_table):
    me = lax.axis_index("dp")
    z, core = me // 2, me % 2
    size = lax.axis_size("dp")
    chips = size // 2
    rows_dev = hidden.shape[0]
    feats, vocab = head_table.shape
    rows = chips * rows_dev
    pair = vocab // TILE // (chips // 2)
    width = (pair // 2 + 1) * TILE

    swap = lambda x: lax.ppermute(x, "dp", [(i, i ^ 1) for i in range(size)])
    side = [2 - 4 * (i % 2) for i in range(size)]
    up = lambda x: lax.ppermute(x, "dp", [(i, (i + side[i]) % size) for i in range(size)])
    down = lambda x: lax.ppermute(x, "dp", [(i, (i - side[i]) % size) for i in range(size)])
    up2 = lambda x: lax.ppermute(x, "dp", [(i, (i + 2 * side[i]) % size) for i in range(size)])
    enc = lambda x: (x * SCALE).astype(WIRE)
    dec = lambda x: x.astype(F32) * (1.0 / SCALE)

    groups = [[c + 2 * k for k in range(chips)] for c in range(2)]
    slices = lax.all_to_all(deal(hidden, chips), "dp", 0, 0, axis_index_groups=groups)
    slices = slices.reshape(rows, 2 * feats)
    head_other = swap(head_table)
    embed_own = embed_table.T
    embed_other = swap(embed_own)
    first, second = slices[:, :feats], slices[:, feats:]
    own = jnp.where(core == 0, first, second)
    others = jnp.where(core == 0, second, first)

    logits = lambda order: logits_of(order, own, others, [head_table, head_other], width)
    far, p3, m3 = logits((4, 3, 5))
    a4, a, b = up2(enc(far)), up(enc(p3)), down(enc(m3))
    p2, m2, p1, m1, p0 = logits((2, 6, 1, 7, 0))
    a = up(enc(p2 + dec(a) + dec(a4)))
    b = down(enc(m2 + dec(b)))
    a = up(enc(p1 + dec(a)))
    b = down(enc(m1 + dec(b)))
    full = add(p0, dec(b)) + dec(a)

    block = softmax_of(full, embed_other)
    tables = [embed_own, embed_other]
    mix = lambda order, blocks, old, **kw: mix_of(order, blocks, tables, [], old, **kw)
    a1, b1 = up(block), down(block)
    *state, za, zb = mix((0,), [block], [])
    a2, b2 = up(a1 + za), down(b1 + zb)
    *state, za, zb = mix((7,), [a1], state)
    a3, b3 = up(a2 + za), down(b2 + zb)
    *state, za, _ = mix((1, 6), [b1, a2], state)
    a4 = up(a3)
    *state, _, _, ready = mix((2, 5), [b2, a3], state, ahead=(3, 4))
    (blocks,) = mix_of((3, 4), [b3, a4], tables, [ready], state)

    result = combine(lax.all_to_all(blocks, "vocab", 0, 0), feats)
    flip = []
    for k in range(chips):
        for c in range(2):
            for r in range(chips):
                for f in range(2):
                    here = (2 * k + c) * size + place(k, r, f)
                    there = (2 * r + c) * size + 2 * k + f
                    flip.append((here, there))
    return lax.ppermute(result, ("dp", "vocab"), flip)


def solution(mesh):
    in_specs = (P("dp", None), P("dp", "vocab"), P("vocab", "dp"))
    out_specs = P("dp", "vocab")
    return jax.shard_map(
        on_device, mesh=mesh, in_specs=in_specs, out_specs=out_specs, check_vma=False
    )
```
